256 devices in a mesh: expert: 32 (over x, y, core), tensor: 8 (over z).
Axes of the slice: x: 4, y: 4, z: 8, core: 2. Of those that a mesh axis runs over, the one named last changes fastest.
Arguments:
- tokens: bfloat16 [32768, 2048], P(('expert', 'tensor')), may hold values from -6 to 6
- cotangent: bfloat16 [32768, 2048], P(('expert', 'tensor')), may hold values from -24 to 24
- router: float32 [2048, 32], replicated, may hold values from -0.0546875 to 0.0546875
- first_choice: int32 [32768], P(('expert', 'tensor')), may hold values from 0 to 31, as said below
- second_choice: int32 [32768], P(('expert', 'tensor')), may hold values from 0 to 31, as said below
- slot_index: int32 [32768], P(('expert', 'tensor')), may hold values from 0 to 3, as said below
- overflow: int32 [32768], P(('expert', 'tensor')), may hold values from 0 to 2, as said below
- weight_in: bfloat16 [32, 2048, 5120], P('expert', None, 'tensor'), may hold values from -0.125 to 0.125
- weight_out: bfloat16 [32, 5120, 2048], P('expert', 'tensor'), may hold values from -0.078125 to 0.078125
Outputs:
- token_grad: bfloat16 [32768, 2048], P(('expert', 'tensor'))
- weight_in_grad: bfloat16 [32, 2048, 5120], P('expert', None, 'tensor')
- weight_out_grad: bfloat16 [32, 5120, 2048], P('expert', 'tensor')
- router_grad: float32 [2048, 32], replicated
The draws below stay inside these ranges and needn't reach their ends.
Inputs may be any that keep to these rules, and one draw needn't show every extreme that they name: `first_choice`: on every device 4 tokens name one common expert as first choice, the same expert on all devices. `second_choice`: never equal to first_choice of the same token. `slot_index`: position among the 4 slots that the token's device has in the expert it goes to (second_choice where overflow is 1); no two live tokens of one device share an expert and a slot; rows placed at second choice take slots after that expert's first-choice rows; 0 for dropped tokens. `overflow`: 1 only where the first choice's 4 slots of the device are taken; 2 where the second choice's are taken as well.
All inputs are finite; a program needn't handle non-finite values.
Results may differ from the reference program's by a relative error of at most 0.019.
Values may be sent and summed in bfloat16 or wider, within the bound.
No kernel may reach another device: no remote copies, remote signals or barrier semaphores. Data moves between devices by JAX's collectives and lax.ppermute only.
A program may use at most 128 MiB of HBM per device.

```python
import jax
import jax.numpy as jnp
from jax import lax

D = 2048
FF = 5120
TOK_DEV = 128
EXPERTS = 32
CAP = 4
TOKENS = 32768
N_TENSOR = 8


def route_tables(key):
    blocks = TOKENS // TOK_DEV
    key_low, key_high, key_order, key_shift, key_force = jax.random.split(key, 5)
    lower = jax.random.randint(key_low, (blocks, TOK_DEV), 0, EXPERTS)
    upper = jax.random.randint(key_high, (blocks, TOK_DEV), 0, EXPERTS)
    ordering = jax.random.permutation(key_order, EXPERTS)
    ranked = jnp.minimum(lower, upper)
    scores = jax.random.randint(key_force, (blocks, TOK_DEV), 0, 1 << 20) * TOK_DEV + jnp.arange(TOK_DEV)[None, :]
    places = jnp.argsort(jnp.argsort(scores, axis=1, stable=True), axis=1, stable=True)
    ranked = jnp.where(places < CAP, 0, ranked)
    first = ordering[ranked]
    shifts = jax.random.randint(key_shift, (blocks, TOK_DEV), 1, EXPERTS)
    second = (first + shifts) % EXPERTS
    labels = jnp.arange(EXPERTS)
    hot_first = (first[:, :, None] == labels[None, None, :]).astype(jnp.int32)
    before_first = jnp.cumsum(hot_first, axis=1) - hot_first
    rank_first = jnp.sum(before_first * hot_first, axis=2)
    placed_first = rank_first < CAP
    used_slots = jnp.minimum(jnp.sum(hot_first, axis=1), CAP)
    match_second = (second[:, :, None] == labels[None, None, :]).astype(jnp.int32)
    hot_second = match_second * (1 - placed_first.astype(jnp.int32))[:, :, None]
    before_second = jnp.cumsum(hot_second, axis=1) - hot_second
    rank_second = jnp.sum(before_second * hot_second, axis=2)
    used_second = jnp.sum(used_slots[:, None, :] * match_second, axis=2)
    placed_second = jnp.logical_and(jnp.logical_not(placed_first), rank_second < CAP - used_second)
    slots = jnp.where(placed_first, rank_first, jnp.where(placed_second, used_second + rank_second, 0))
    flags = jnp.where(placed_first, 0, jnp.where(placed_second, 1, 2))
    return (first.reshape(-1).astype(jnp.int32), second.reshape(-1).astype(jnp.int32), slots.reshape(-1).astype(jnp.int32), flags.reshape(-1).astype(jnp.int32))


def draw_first_choice(key, part):
    tables = route_tables(key)
    return tables[0]


def draw_second_choice(key, part):
    tables = route_tables(key)
    return tables[1]


def draw_slot_index(key, part):
    tables = route_tables(key)
    return tables[2]


def draw_overflow(key, part):
    tables = route_tables(key)
    return tables[3]


def level_of(key, dims, cuts, least, largest):
    def one(position, parts):
        draws = jax.random.uniform(jax.random.fold_in(jax.random.fold_in(key, 6), position), (parts,), jnp.float32, least / len(cuts), largest / len(cuts))
        return jnp.repeat(jnp.exp(draws), dims[position] // parts).reshape((-1,) + (1,) * (len(dims) - position - 1))

    loudness = one(*cuts[0])
    for cut in cuts[1:]:
        loudness = loudness * one(*cut)
    return loudness


def normal_values(rng, extent, spread, limit, shards=(), kind=jnp.bfloat16):
    array = spread * jax.random.normal(rng, extent, jnp.float32)
    if shards:
        array = array * level_of(rng, extent, shards, -0.22, 0.18)
    return jnp.clip(array, -limit, limit).astype(kind)


def setup_inputs(seed: int = 0) -> dict:
    arg_keys = jax.random.split(jax.random.key(seed), 10)
    return {
        "tokens": normal_values(arg_keys[0], (TOKENS, D), 1.0, 6.0, ((0, 256),)),
        "cotangent": normal_values(arg_keys[1], (TOKENS, D), 4.0, 24.0, ((0, 256),)),
        "router": normal_values(arg_keys[2], (D, EXPERTS), (6 * D) ** -0.5, 0.0546875, (), jnp.float32),
        "first_choice": draw_first_choice(jax.random.fold_in(arg_keys[9], 71), 0),
        "second_choice": draw_second_choice(jax.random.fold_in(arg_keys[9], 71), 0),
        "slot_index": draw_slot_index(jax.random.fold_in(arg_keys[9], 71), 0),
        "overflow": draw_overflow(jax.random.fold_in(arg_keys[9], 71), 0),
        "weight_in": normal_values(arg_keys[7], (EXPERTS, D, FF), D ** -0.5, 0.125, ((0, 32), (2, 8))),
        "weight_out": normal_values(arg_keys[8], (EXPERTS, FF, D), FF ** -0.5, 0.078125, ((0, 32), (1, 8))),
    }


def gelu_parts(hidden):
    curve = jnp.tanh(0.7978845608 * (hidden + 0.044715 * hidden * hidden * hidden))
    shaped = 0.5 * hidden * (1.0 + curve)
    slope = 0.5 * (1.0 + curve) + 0.5 * hidden * (1.0 - curve * curve) * 0.7978845608 * (1.0 + 0.134145 * hidden * hidden)
    return shaped, slope


def blockwise(operand, matrix_rows):
    piece_size = FF // N_TENSOR
    summed = jnp.zeros((operand.shape[0], matrix_rows.shape[1]), jnp.float32)
    for member in range(N_TENSOR):
        portion = jnp.dot(operand[:, member * piece_size:(member + 1) * piece_size], matrix_rows[member * piece_size:(member + 1) * piece_size], preferred_element_type=jnp.float32)
        portion = lax.optimization_barrier(portion.astype(jnp.bfloat16))
        summed = summed + portion.astype(jnp.float32)
    return summed.astype(jnp.bfloat16)


def one_expert(inputs):
    rows_in, rows_grad, matrix_in, matrix_out = inputs
    hidden = jnp.dot(rows_in, matrix_in, preferred_element_type=jnp.float32)
    shaped, slope = gelu_parts(hidden)
    activated = shaped.astype(jnp.bfloat16)
    outputs = blockwise(activated, matrix_out)
    act_grad = jnp.dot(rows_grad, matrix_out.T, preferred_element_type=jnp.float32)
    out_weight_grad = jnp.dot(activated.T, rows_grad, preferred_element_type=jnp.float32).astype(jnp.bfloat16)
    hidden_grad = (act_grad * slope).astype(jnp.bfloat16)
    in_weight_grad = jnp.dot(rows_in.T, hidden_grad, preferred_element_type=jnp.float32).astype(jnp.bfloat16)
    input_grad = blockwise(hidden_grad, matrix_in.T)
    return outputs, input_grad, in_weight_grad, out_weight_grad


def reference(tokens, cotangent, router, first_choice, second_choice, slot_index, overflow, weight_in, weight_out):
    logits = jnp.dot(tokens.astype(jnp.float32), router, precision=lax.Precision.HIGHEST)
    raised = jnp.exp(logits)
    chances = raised / jnp.sum(raised, axis=1, keepdims=True)
    chosen = jnp.where(overflow == 0, first_choice, second_choice).astype(jnp.int32)
    is_live = overflow < 2
    chosen_hot = (chosen[:, None] == jnp.arange(EXPERTS, dtype=jnp.int32)[None, :]).astype(jnp.float32)
    chosen_chance = jnp.sum(chances * chosen_hot, axis=1)
    gate_value = jnp.where(is_live, chosen_chance, jnp.float32(0.0))
    scaled_cot = (gate_value[:, None] * cotangent.astype(jnp.float32)).astype(jnp.bfloat16)
    per_expert = (TOKENS // TOK_DEV) * CAP
    source_device = (jnp.arange(TOKENS, dtype=jnp.int32) // TOK_DEV).astype(jnp.int32)
    target = (chosen * per_expert + source_device * CAP + slot_index).astype(jnp.int32)
    target = jnp.where(is_live, target, EXPERTS * per_expert).astype(jnp.int32)
    empty_rows = jnp.zeros((EXPERTS * per_expert, D), jnp.bfloat16)
    rows_x = empty_rows.at[target].set(tokens, mode="drop").reshape(EXPERTS, per_expert, D)
    rows_dy = empty_rows.at[target].set(scaled_cot, mode="drop").reshape(EXPERTS, per_expert, D)
    outputs, input_grads, weight_in_grad, weight_out_grad = lax.map(one_expert, (rows_x, rows_dy, weight_in, weight_out))
    safe_target = jnp.minimum(target, EXPERTS * per_expert - 1).astype(jnp.int32)
    token_out = jnp.where(is_live[:, None], outputs.reshape(-1, D)[safe_target].astype(jnp.float32), jnp.float32(0.0))
    token_back = jnp.where(is_live[:, None], input_grads.reshape(-1, D)[safe_target].astype(jnp.float32), jnp.float32(0.0))
    gate_grad = jnp.sum(token_out * cotangent.astype(jnp.float32), axis=1)
    logit_grad = jnp.where(is_live, chosen_chance * gate_grad, jnp.float32(0.0))[:, None] * (chosen_hot - chances)
    token_grad = (token_back + jnp.dot(logit_grad, router.T, precision=lax.Precision.HIGHEST)).astype(jnp.bfloat16)
    router_grad = jnp.dot(tokens.astype(jnp.float32).T, logit_grad, precision=lax.Precision.HIGHEST)
    return token_grad, weight_in_grad, weight_out_grad, router_grad
```

```python
import jax
import jax.numpy as jnp
from jax import lax
from jax.sharding import PartitionSpec as P

RING = 8
HIGH = lax.Precision.HIGHEST


def gelu_parts(hidden):
    curve = jnp.tanh(0.7978845608 * (hidden + 0.044715 * hidden * hidden * hidden))
    shaped = 0.5 * hidden * (1.0 + curve)
    slope = 0.5 * (1.0 + curve) + 0.5 * hidden * (1.0 - curve * curve) * 0.7978845608 * (
        1.0 + 0.134145 * hidden * hidden
    )
    return (shaped, slope)


def contract_first(operand, other):
    return lax.dot_general(
        operand, other, (((0,), (0,)), ((), ())), preferred_element_type=jnp.float32
    )


def contract_last(operand, other):
    return lax.dot_general(
        operand, other, (((1,), (1,)), ((), ())), preferred_element_type=jnp.float32
    )


def upward(value):
    return lax.ppermute(value, "tensor", [(i, (i + 1) % RING) for i in range(RING)])


def downward(value):
    return lax.ppermute(value, "tensor", [(i, (i - 1) % RING) for i in range(RING)])


def swap(value):
    return lax.all_to_all(value, "expert", split_axis=0, concat_axis=0, tiled=True)


def split_two(value):
    high = value.astype(jnp.bfloat16)
    low = (value - high.astype(jnp.float32)).astype(jnp.bfloat16)
    return high, low


def ring_gather(block):
    half = block.shape[0] // 2
    parts = [block] + [None] * (RING - 1)
    up = down = block
    for step in range(1, RING // 2):
        up, down = upward(up), downward(down)
        parts[RING - step], parts[step] = up, down
    parts[RING // 2] = jnp.concatenate([upward(up[:half]), downward(down[half:])], 0)
    return parts


def ring_scatter(parts):
    half = parts[0].shape[0] // 2
    up = upward(parts[4][:half])
    down = downward(parts[4][half:])
    up = jnp.concatenate([up + parts[3][:half], parts[3][half:]], 0)
    down = jnp.concatenate([parts[5][:half], down + parts[5][half:]], 0)
    up = upward(up) + parts[2]
    down = downward(down) + parts[6]
    up = upward(up) + parts[1]
    down = downward(down) + parts[7]
    total = (
        upward(up).astype(jnp.float32)
        + downward(down).astype(jnp.float32)
        + parts[0].astype(jnp.float32)
    )
    return total.astype(jnp.bfloat16)


def on_device(
    tokens,
    cotangent,
    router,
    first_choice,
    second_choice,
    slot_index,
    overflow,
    weight_in,
    weight_out,
):
    expert_count = router.shape[1]
    token_count = tokens.shape[0]
    model_width = tokens.shape[1]
    capacity = token_count // expert_count
    slots = expert_count * capacity
    matrix_in = weight_in[0]
    matrix_out = weight_out[0]
    own_hot = (jnp.arange(expert_count) == lax.axis_index("expert")).astype(jnp.float32)[None, :]
    chosen = jnp.where(overflow == 0, first_choice, second_choice)
    position = jnp.where(overflow < 2, chosen * capacity + slot_index, -1)
    place = (jnp.arange(slots)[:, None] == position[None, :]).astype(jnp.bfloat16)

    def send_rows(rows):
        placed = jnp.dot(place, rows, preferred_element_type=jnp.float32).astype(jnp.bfloat16)
        arrived = swap(placed.reshape(expert_count, capacity, model_width))
        return arrived.reshape(slots, model_width)

    rows_x = ring_gather(send_rows(tokens))
    rows_cot = ring_gather(send_rows(cotangent))

    router_high, router_low = split_two(router)
    matrix_back = jnp.concatenate([matrix_in, router_high, router_high, router_low], 1)

    kept = []
    back = [None] * RING
    for members in ((0, 1, 7), (2, 6), (3, 5), (4,)):
        x = jnp.concatenate([rows_x[j] for j in members], 0)
        cot = jnp.concatenate([rows_cot[j] for j in members], 0)
        logits = jnp.dot(x.astype(jnp.float32), router, precision=HIGH)
        raised = jnp.exp(logits)
        chances = raised / jnp.sum(raised, axis=1, keepdims=True)
        gate = jnp.sum(chances * own_hot, axis=1, keepdims=True)
        scaled = (gate * cot.astype(jnp.float32)).astype(jnp.bfloat16)
        shaped, slope = gelu_parts(jnp.dot(x, matrix_in, preferred_element_type=jnp.float32))
        activated = shaped.astype(jnp.bfloat16)
        act_grad = contract_last(scaled, matrix_out)
        strength = jnp.sum(activated.astype(jnp.float32) * act_grad, axis=1, keepdims=True)
        hidden_grad = (act_grad * slope).astype(jnp.bfloat16)
        logit_high, logit_low = split_two(strength * (own_hot - chances))
        widened = jnp.concatenate([hidden_grad, logit_high, logit_low, logit_high], 1)
        term = contract_last(widened, matrix_back).astype(jnp.bfloat16)
        for n, j in enumerate(members):
            back[j] = term[n * slots : (n + 1) * slots]
        kept.append((x, scaled, activated, hidden_grad, jnp.concatenate([logit_high, logit_low], 1)))

    x, scaled, activated, hidden_grad, logit_grad = (
        jnp.concatenate([group[i] for group in kept], 0) for i in range(5)
    )

    router_term = contract_first(logit_grad, x)
    router_term = router_term[:expert_count] + router_term[expert_count:]
    lanes = model_width // 16
    router_term = (
        router_term.reshape(2, expert_count // 2, 16, lanes)
        .transpose(2, 0, 1, 3)
        .reshape(expert_count, expert_count // 2, lanes)
    )
    router_sum = jnp.sum(swap(router_term), axis=0)
    for mask in (1, 2, 4):
        router_sum = router_sum + lax.ppermute(
            router_sum, "tensor", [(i, i ^ mask) for i in range(RING)]
        )
    spread = swap(jnp.broadcast_to(router_sum[None], (expert_count,) + router_sum.shape))
    router_grad = (
        spread.reshape(16, 2, expert_count // 2, lanes)
        .transpose(1, 2, 0, 3)
        .reshape(expert_count, model_width)
        .T
    )

    own = ring_scatter(back)
    home = swap(own.reshape(expert_count, capacity, model_width)).reshape(slots, model_width)
    token_grad = contract_first(place, home).astype(jnp.bfloat16)

    weight_out_grad = contract_first(activated, scaled).astype(jnp.bfloat16)[None]
    weight_in_grad = contract_first(x, hidden_grad).astype(jnp.bfloat16)[None]
    return (token_grad, weight_in_grad, weight_out_grad, router_grad)


def solution(mesh):
    in_specs = (
        P(("expert", "tensor"), None),
        P(("expert", "tensor"), None),
        P(),
        P(("expert", "tensor")),
        P(("expert", "tensor")),
        P(("expert", "tensor")),
        P(("expert", "tensor")),
        P("expert", None, "tensor"),
        P("expert", "tensor", None),
    )
    out_specs = (
        P(("expert", "tensor"), None),
        P("expert", None, "tensor"),
        P("expert", "tensor", None),
        P(),
    )
    return jax.shard_map(
        on_device, mesh=mesh, in_specs=in_specs, out_specs=out_specs, check_vma=False
    )
```

```python
import functools

import jax
import jax.numpy as jnp
from jax import lax
from jax.experimental import pallas as pl
from jax.experimental.pallas import tpu as pltpu
from jax.sharding import PartitionSpec as P

RING = 8
LANES = 128


def gelu_parts(hidden):
    curve = jnp.tanh(0.7978845608 * (hidden + 0.044715 * hidden * hidden * hidden))
    shaped = 0.5 * hidden * (1.0 + curve)
    slope = 0.5 * (1.0 + curve) + 0.5 * hidden * (1.0 - curve * curve) * 0.7978845608 * (
        1.0 + 0.134145 * hidden * hidden
    )
    return (shaped, slope)


def contract_first(operand, other):
    return lax.dot_general(
        operand, other, (((0,), (0,)), ((), ())), preferred_element_type=jnp.float32
    )


def contract_last(operand, other):
    return lax.dot_general(
        operand, other, (((1,), (1,)), ((), ())), preferred_element_type=jnp.float32
    )


def upward(value):
    return lax.ppermute(value, "tensor", [(i, (i + 1) % RING) for i in range(RING)])


def downward(value):
    return lax.ppermute(value, "tensor", [(i, (i - 1) % RING) for i in range(RING)])


def swap(value):
    return lax.all_to_all(value, "expert", split_axis=0, concat_axis=0, tiled=True)


def split_two(value):
    high = value.astype(jnp.bfloat16)
    low = (value - high.astype(jnp.float32)).astype(jnp.bfloat16)
    return high, low


def group_kernel(
    plan, first, row_start, capacity, *refs
):
    count = len(plan)
    refs = list(refs)

    def take(n):
        out = refs[:n]
        del refs[:n]
        return out

    blocks = take(sum(1 if kind == "pair" else 2 for kind in plan))
    router_wide, router_back, hot_first, hot_all, win, wout = take(6)
    if not first:
        (rt_prev,) = take(1)
        take(4)
    backs = take(sum(1 if kind == "pair" else 2 for kind in plan))
    rt_out, x_all, dy_all, act_all, hg_all = take(5)
    xs, dys, acts, hgl, winr, wouts, in_sems, out_sems = refs
    rows = xs.shape[0]
    each = rows // count
    hidden_units = wouts.shape[0]
    width = xs.shape[1]

    fetch = [
        pltpu.make_async_copy(win, winr.at[:, pl.ds(0, hidden_units)], in_sems.at[0]),
        pltpu.make_async_copy(router_back, winr.at[:, pl.ds(hidden_units, LANES)], in_sems.at[1]),
        pltpu.make_async_copy(wout, wouts, in_sems.at[2]),
    ]
    for copy in fetch:
        copy.start()

    cots = []
    at = 0
    for n, kind in enumerate(plan):
        if kind == "pair":
            xs[n * each : (n + 1) * each, :] = blocks[at][0:each, :]
            cots.append((blocks[at], each))
            at += 1
        else:
            xs[n * each : (n + 1) * each, :] = blocks[at][...]
            cots.append((blocks[at + 1], 0))
            at += 2

    wide = jnp.dot(xs[...], router_wide[...], preferred_element_type=jnp.float32)
    raised = jnp.exp(wide[:, :LANES] + wide[:, LANES:])
    total = jnp.sum(raised, axis=1, keepdims=True) * (capacity / LANES)
    chances = raised / total
    gate = jnp.sum(chances * hot_first[...], axis=1, keepdims=True)
    for n, (ref, offset) in enumerate(cots):
        dys[n * each : (n + 1) * each, :] = (
            gate[n * each : (n + 1) * each] * ref[offset : offset + each, :].astype(jnp.float32)
        ).astype(jnp.bfloat16)

    for copy in fetch:
        copy.wait()

    strength = jnp.zeros((rows, 1), jnp.float32)
    start = 0
    while start < hidden_units:
        size = min(256, hidden_units - start)
        span = slice(start, start + size)
        shaped, slope = gelu_parts(
            jnp.dot(xs[...], winr[:, span], preferred_element_type=jnp.float32)
        )
        activated = shaped.astype(jnp.bfloat16)
        act_grad = contract_last(dys[...], wouts[span, :])
        acts[:, span] = activated
        hgl[:, span] = (act_grad * slope).astype(jnp.bfloat16)
        strength = strength + jnp.sum(
            activated.astype(jnp.float32) * act_grad, axis=1, keepdims=True
        )
        start += size

    logit_grad = strength * (hot_all[...] - chances)
    high = logit_grad.astype(jnp.bfloat16)
    high_wide = high.astype(jnp.float32)
    low_wide = logit_grad - high_wide
    lane = lax.broadcasted_iota(jnp.int32, (rows, LANES), 1)
    piece = lane // capacity
    joined = jnp.where(piece == 1, low_wide, jnp.where(piece == 3, 0.0, high_wide))
    hgl[:, hidden_units:] = joined.astype(jnp.bfloat16)

    stores = [
        pltpu.make_async_copy(src, dst.at[pl.ds(row_start, rows), :], out_sems.at[i])
        for i, (src, dst) in enumerate(
            (
                (xs, x_all),
                (dys, dy_all),
                (acts, act_all),
                (hgl.at[:, pl.ds(0, hidden_units)], hg_all),
            )
        )
    ]
    for copy in stores:
        copy.start()

    for start in range(0, width, 256):
        span = slice(start, start + 256)
        term = contract_last(hgl[...], winr[span, :]).astype(jnp.bfloat16)
        at = 0
        for n, kind in enumerate(plan):
            if kind == "pair":
                backs[at][:, span] = term[n * each : (n + 1) * each]
                at += 1
            else:
                middle = n * each + each // 2
                backs[at][:, span] = term[n * each : middle]
                backs[at + 1][:, span] = term[middle : (n + 1) * each]
                at += 2

    half = capacity // 2
    for start in range(0, width, 256):
        both = contract_first(hgl[:, hidden_units:], xs[:, start : start + 256])
        part = both[:capacity] + both[capacity : 2 * capacity]
        for extra in range(2):
            for side in range(2):
                slot = (start // LANES + extra) * 2 + side
                value = part[
                    side * half : (side + 1) * half, extra * LANES : (extra + 1) * LANES
                ]
                if not first:
                    value = value + rt_prev[slot]
                rt_out[slot] = value

    for copy in stores:
        copy.wait()


def run_group(plan, blocks, constants, weights, carry, row_start, experts):
    each = blocks[0].shape[0] // 2
    width = blocks[0].shape[1]
    hidden_units = weights[1].shape[0]
    rows = each * len(plan)
    total = RING * each * 2
    bf = jnp.bfloat16
    back_shapes = []
    for kind in plan:
        if kind == "pair":
            back_shapes.append(jax.ShapeDtypeStruct((each, width), bf))
        else:
            back_shapes += [jax.ShapeDtypeStruct((each // 2, width), bf)] * 2
    out_shape = back_shapes + [
        jax.ShapeDtypeStruct((experts, experts // 2, LANES), jnp.float32),
        jax.ShapeDtypeStruct((total, width), bf),
        jax.ShapeDtypeStruct((total, width), bf),
        jax.ShapeDtypeStruct((total, hidden_units), bf),
        jax.ShapeDtypeStruct((total, hidden_units), bf),
    ]
    vmem = pl.BlockSpec(memory_space=pltpu.VMEM)
    anyw = pl.BlockSpec(memory_space=pl.ANY)
    operands = list(blocks) + list(constants) + list(weights)
    in_specs = [vmem] * len(blocks) + [vmem, anyw, vmem, vmem, anyw, anyw]
    aliases = {}
    first = carry is None
    if not first:
        base = len(operands)
        operands += list(carry)
        in_specs += [vmem] + [anyw] * 4
        aliases = {base + 1 + i: len(back_shapes) + 1 + i for i in range(4)}
    out_specs = [vmem] * (len(back_shapes) + 1) + [anyw] * 4
    flops = 2 * rows * width * (hidden_units * 3 + 512)
    out = pl.pallas_call(
        functools.partial(group_kernel, plan, first, row_start, experts),
        out_shape=out_shape,
        in_specs=in_specs,
        out_specs=out_specs,
        input_output_aliases=aliases,
        scratch_shapes=[
            pltpu.VMEM((rows, width), bf),
            pltpu.VMEM((rows, width), bf),
            pltpu.VMEM((rows, hidden_units), bf),
            pltpu.VMEM((rows, hidden_units + LANES), bf),
            pltpu.VMEM((width, hidden_units + LANES), bf),
            pltpu.VMEM((hidden_units, width), bf),
            pltpu.SemaphoreType.DMA((3,)),
            pltpu.SemaphoreType.DMA((4,)),
        ],
        compiler_params=pltpu.CompilerParams(vmem_limit_bytes=40 * 1024 * 1024),
        cost_estimate=pl.CostEstimate(
            flops=flops, bytes_accessed=12 * 1024 * 1024, transcendentals=rows * hidden_units
        ),
    )(*operands)
    return out[: len(back_shapes)], out[len(back_shapes) :]


def on_device(
    tokens,
    cotangent,
    router,
    first_choice,
    second_choice,
    slot_index,
    overflow,
    weight_in,
    weight_out,
):
    experts = router.shape[1]
    token_count, width = tokens.shape
    capacity = token_count // experts
    slots = experts * capacity
    half = capacity // 2
    each = experts * half
    bf = jnp.bfloat16
    matrix_in = weight_in[0]
    matrix_out = weight_out[0]

    chosen = jnp.where(overflow == 0, first_choice, second_choice)
    position = jnp.where(overflow < 2, chosen * capacity + slot_index, -1)
    place = (jnp.arange(slots)[:, None] == position[None, :]).astype(bf)

    row = jnp.arange(slots)
    streams = []
    for stream in range(2):
        wanted = (row // capacity) * capacity + stream * half + row % half
        is_token = (row % capacity) < half
        hit = wanted[:, None] == position[None, :]
        take_tokens = jnp.logical_and(hit, is_token[:, None]).astype(bf)
        take_cot = jnp.logical_and(hit, jnp.logical_not(is_token)[:, None]).astype(bf)
        packed = (
            jnp.dot(take_tokens, tokens, preferred_element_type=jnp.float32)
            + jnp.dot(take_cot, cotangent, preferred_element_type=jnp.float32)
        ).astype(bf)
        arrived = swap(packed.reshape(experts, capacity, width))
        streams.append(
            arrived.reshape(experts, 2, half, width).transpose(1, 0, 2, 3).reshape(slots, width)
        )

    router_high, router_low = split_two(router)
    router_wide = jnp.concatenate([router_high] * 4 + [router_low] * 4, 1)
    router_back = jnp.concatenate(
        [router_high, router_high, router_low, jnp.zeros_like(router_low)], 1
    )
    lane = jnp.arange(LANES)
    me = lax.axis_index("expert")
    hot_first = (lane == me).astype(jnp.float32)[None, :]
    hot_all = (lane % experts == me).astype(jnp.float32)[None, :]
    constants = (router_wide, router_back, hot_first, hot_all)
    weights = (matrix_in, matrix_out)

    near, far, last = [], [], []
    for own in streams:
        up1, down1 = upward(own), downward(own)
        up2, down2 = upward(up1), downward(down1)
        up3, down3 = upward(up2), downward(down2)
        near.append((own, down1, up1, down2, up2))
        far.append((down3, up3, upward(up3[:each]), downward(down3[each:])))

    carry = None
    backs_near, backs_far = [], []
    row_start = 0
    for stream in range(2):
        out, carry = run_group(
            ("pair",) * 5, near[stream], constants, weights, carry, row_start, experts
        )
        backs_near.append(out)
        row_start += 5 * each
    for stream in range(2):
        out, carry = run_group(
            ("pair", "pair", "halves"), far[stream], constants, weights, carry, row_start, experts
        )
        backs_far.append(out)
        row_start += 3 * each
    router_term, x, scaled, activated, hidden_grad = carry

    router_sum = jnp.sum(swap(router_term), axis=0)
    for mask in (1, 2, 4):
        router_sum = router_sum + lax.ppermute(
            router_sum, "tensor", [(i, i ^ mask) for i in range(RING)]
        )

    owns = []
    for stream in range(2):
        b0, b1, b7, b2, b6 = backs_near[stream]
        b3, b5, b4_up, b4_down = backs_far[stream]
        cut = each // 2
        up, down = upward(b4_up), downward(b4_down)
        up = jnp.concatenate([up + b3[:cut], b3[cut:]], 0)
        down = jnp.concatenate([b5[:cut], down + b5[cut:]], 0)
        up = upward(up) + b2
        down = downward(down) + b6
        up = upward(up) + b1
        down = downward(down) + b7
        total = (
            upward(up).astype(jnp.float32)
            + downward(down).astype(jnp.float32)
            + b0.astype(jnp.float32)
        )
        owns.append(total.astype(bf).reshape(experts, half, width))

    sum_high, sum_low = split_two(router_sum)
    sums = [
        jnp.broadcast_to(part.reshape(1, 1, width), (experts, 1, width))
        for part in (sum_high, sum_low)
    ]
    home = swap(jnp.concatenate(owns + sums, 1))
    token_grad = contract_first(place, home[:, :capacity].reshape(slots, width)).astype(bf)
    spread = home[:, capacity].astype(jnp.float32) + home[:, capacity + 1].astype(jnp.float32)
    router_grad = (
        spread.reshape(width // LANES, 2, experts // 2, LANES)
        .transpose(0, 3, 1, 2)
        .reshape(width, experts)
    )

    weight_out_grad = contract_first(activated, scaled).astype(bf)[None]
    weight_in_grad = contract_first(x, hidden_grad).astype(bf)[None]
    return (token_grad, weight_in_grad, weight_out_grad, router_grad)


def solution(mesh):
    in_specs = (
        P(("expert", "tensor"), None),
        P(("expert", "tensor"), None),
        P(),
        P(("expert", "tensor")),
        P(("expert", "tensor")),
        P(("expert", "tensor")),
        P(("expert", "tensor")),
        P("expert", None, "tensor"),
        P("expert", "tensor", None),
    )
    out_specs = (
        P(("expert", "tensor"), None),
        P("expert", None, "tensor"),
        P("expert", "tensor", None),
        P(),
    )
    return jax.shard_map(
        on_device, mesh=mesh, in_specs=in_specs, out_specs=out_specs, check_vma=False
    )
```

```python
import functools

import jax
import jax.numpy as jnp
from jax import lax
from jax.experimental import pallas as pl
from jax.experimental.pallas import tpu as pltpu
from jax.sharding import PartitionSpec as P

RING = 8
LANES = 128


def gelu_parts(hidden):
    curve = jnp.tanh(0.7978845608 * (hidden + 0.044715 * hidden * hidden * hidden))
    shaped = 0.5 * hidden * (1.0 + curve)
    slope = 0.5 * (1.0 + curve) + 0.5 * hidden * (1.0 - curve * curve) * 0.7978845608 * (
        1.0 + 0.134145 * hidden * hidden
    )
    return (shaped, slope)


def contract_first(operand, other):
    return lax.dot_general(
        operand, other, (((0,), (0,)), ((), ())), preferred_element_type=jnp.float32
    )


def contract_last(operand, other):
    return lax.dot_general(
        operand, other, (((1,), (1,)), ((), ())), preferred_element_type=jnp.float32
    )


def upward(value):
    return lax.ppermute(value, "tensor", [(i, (i + 1) % RING) for i in range(RING)])


def downward(value):
    return lax.ppermute(value, "tensor", [(i, (i - 1) % RING) for i in range(RING)])


def swap(value):
    return lax.all_to_all(value, "expert", split_axis=0, concat_axis=0, tiled=True)


def group_kernel(
    places,
    first,
    row_start,
    experts,
    *refs,
):
    refs = list(refs)
    count = len(places)

    def take(n):
        out = refs[:n]
        del refs[:n]
        return out

    x_parts, cot_parts = take(count), take(count)
    me, router_rows, hot_first, hot_all, win, wout = take(6)
    if not first:
        (rt_prev,) = take(1)
        take(5)
    flag, rt_out, x_all, dy_all, act_all, hg_all, back_all = take(7)
    if first:
        win_far, wout_far = win, wout
        win, wout = take(2)
    xs, cots, dys, acts, hgs, terms, router_wide, router_back, in_sems, out_sems = refs
    rows, width = xs.shape
    each = rows // count
    hidden_units = acts.shape[1]

    def part(n):
        return slice(n * each, (n + 1) * each)

    fetch_x = [
        pltpu.make_async_copy(x_parts[n], xs.at[pl.ds(n * each, each), :], in_sems.at[n])
        for n in range(count)
    ]
    fetch_cot = [
        pltpu.make_async_copy(
            cot_parts[n], cots.at[pl.ds(n * each, each), :], in_sems.at[count + n]
        )
        for n in range(count)
    ]
    fetch_weights = []
    if first:
        fetch_weights = [
            pltpu.make_async_copy(win_far, win, in_sems.at[2 * count]),
            pltpu.make_async_copy(wout_far, wout, in_sems.at[2 * count + 1]),
        ]
    for copy in fetch_x + fetch_cot + fetch_weights:
        copy.start()
    flag[...] = jnp.zeros(flag.shape, flag.dtype)
    whole = router_rows[...]
    high = whole.astype(jnp.bfloat16)
    low = (whole - high.astype(jnp.float32)).astype(jnp.bfloat16)
    for n in range(LANES // experts):
        router_wide[n * experts : (n + 1) * experts, :] = high
        router_wide[LANES + n * experts : LANES + (n + 1) * experts, :] = low
        router_back[n * experts : (n + 1) * experts, :] = (high, high, low, jnp.zeros_like(low))[n]

    for copy in fetch_x:
        copy.wait()
    wide = contract_last(xs[...], router_wide[...])
    raised = jnp.exp(wide[:, :LANES] + wide[:, LANES:])
    total = jnp.sum(raised, axis=1, keepdims=True) * (experts / LANES)
    chances = raised / total
    gate = jnp.sum(chances * hot_first[...], axis=1, keepdims=True)
    for copy in fetch_cot:
        copy.wait()
    dys[...] = (gate * cots[...].astype(jnp.float32)).astype(jnp.bfloat16)

    for copy in fetch_weights:
        copy.wait()
    strength = jnp.zeros((rows, 1), jnp.float32)
    start = 0
    while start < hidden_units:
        span = slice(start, min(start + 256, hidden_units))
        shaped, slope = gelu_parts(
            jnp.dot(xs[...], win[:, span], preferred_element_type=jnp.float32)
        )
        activated = shaped.astype(jnp.bfloat16)
        act_grad = contract_last(dys[...], wout[span, :])
        acts[:, span] = activated
        hgs[:, span] = (act_grad * slope).astype(jnp.bfloat16)
        strength = strength + jnp.sum(
            activated.astype(jnp.float32) * act_grad, axis=1, keepdims=True
        )
        start += 256

    stores = [
        pltpu.make_async_copy(src, dst.at[pl.ds(row_start, rows), :], out_sems.at[i])
        for i, (src, dst) in enumerate(
            ((xs, x_all), (dys, dy_all), (acts, act_all), (hgs, hg_all))
        )
    ]
    for copy in stores:
        copy.start()

    logit_grad = strength * (hot_all[...] - chances)
    high_wide = logit_grad.astype(jnp.bfloat16).astype(jnp.float32)
    piece = lax.broadcasted_iota(jnp.int32, (rows, LANES), 1) // experts
    joined = jnp.where(
        piece == 1, logit_grad - high_wide, jnp.where(piece == 3, 0.0, high_wide)
    ).astype(jnp.bfloat16)

    for start in range(0, width, 256):
        span = slice(start, start + 256)
        term = contract_last(hgs[...], win[span, :]) + jnp.dot(
            joined, router_back[:, span], preferred_element_type=jnp.float32
        )
        terms[:, span] = term.astype(jnp.bfloat16)

    block = x_all.shape[0] // RING
    for n, (ahead, offset) in enumerate(places):
        at = pl.multiple_of(lax.rem(me[0] + ahead, RING) * block + offset, each)
        stores.append(
            pltpu.make_async_copy(
                terms.at[pl.ds(n * each, each), :],
                back_all.at[pl.ds(at, each), :],
                out_sems.at[4 + n],
            )
        )
        stores[-1].start()

    half = experts // 2
    for start in range(0, width, 256):
        both = contract_first(joined, xs[:, start : start + 256])
        summed = both[:experts] + both[experts : 2 * experts]
        for extra in range(2):
            for side in range(2):
                slot = (start // LANES + extra) * 2 + side
                value = summed[
                    side * half : (side + 1) * half, extra * LANES : (extra + 1) * LANES
                ]
                if not first:
                    value = value + rt_prev[slot]
                rt_out[slot] = value

    for copy in stores:
        copy.wait()


def run_group(x_parts, cot_parts, places, shared, carry, row_start, total_rows):
    _, router_rows, _, _, win, wout = shared
    count = len(x_parts)
    experts, width = router_rows.shape
    hidden_units = win.shape[1]
    rows = count * x_parts[0].shape[0]
    bf = jnp.bfloat16
    out_shape = [
        jax.ShapeDtypeStruct((8, LANES), jnp.float32),
        pltpu.VMEM((experts, experts // 2, LANES), jnp.float32),
        pltpu.HBM((total_rows, width), bf),
        pltpu.HBM((total_rows, width), bf),
        pltpu.HBM((total_rows, hidden_units), bf),
        pltpu.HBM((total_rows, hidden_units), bf),
        pltpu.HBM((total_rows, width), bf),
    ]
    vmem = pl.BlockSpec(memory_space=pltpu.VMEM)
    hbm = pl.BlockSpec(memory_space=pltpu.HBM)
    first = carry is None
    parts = (*x_parts, *cot_parts)
    space = pltpu.VMEM if first else pltpu.HBM
    parts = [pltpu.with_memory_space_constraint(part, space) for part in parts]
    operands = [*parts, *shared]
    in_specs = [vmem if first else hbm] * (2 * count)
    in_specs += [pl.BlockSpec(memory_space=pltpu.SMEM), vmem, vmem, vmem]
    in_specs += [hbm if first else vmem] * 2
    out_specs = [vmem, vmem] + [hbm] * 5
    aliases = {}
    if first:
        out_shape += [pltpu.VMEM(win.shape, bf), pltpu.VMEM(wout.shape, bf)]
        out_specs += [vmem, vmem]
    else:
        base = len(operands)
        operands.append(carry[0])
        operands += [pltpu.with_memory_space_constraint(part, pltpu.HBM) for part in carry[1:]]
        in_specs += [vmem] + [hbm] * 5
        aliases = {base + 1 + i: 2 + i for i in range(5)}
    out = pl.pallas_call(
        functools.partial(group_kernel, places, first, row_start, experts),
        out_shape=out_shape,
        in_specs=in_specs,
        out_specs=out_specs,
        input_output_aliases=aliases,
        scratch_shapes=[
            pltpu.VMEM((rows, width), bf),
            pltpu.VMEM((rows, width), bf),
            pltpu.VMEM((rows, width), bf),
            pltpu.VMEM((rows, hidden_units), bf),
            pltpu.VMEM((rows, hidden_units), bf),
            pltpu.VMEM((rows, width), bf),
            pltpu.VMEM((2 * LANES, width), bf),
            pltpu.VMEM((LANES, width), bf),
            pltpu.SemaphoreType.DMA((2 * count + 2,)),
            pltpu.SemaphoreType.DMA((4 + count,)),
        ],
        compiler_params=pltpu.CompilerParams(vmem_limit_bytes=16 * 1024 * 1024),
        cost_estimate=pl.CostEstimate(
            flops=2 * rows * width * (hidden_units * 3 + 512),
            bytes_accessed=4 * 1024 * 1024,
            transcendentals=rows * hidden_units,
        ),
    )(*operands)
    return out[0], out[1:7], out[7:]


def gate(values, *earlier):
    hbm = pl.BlockSpec(memory_space=pltpu.HBM)
    return pl.pallas_call(
        lambda *refs: None,
        out_shape=[jax.ShapeDtypeStruct(value.shape, value.dtype) for value in values],
        in_specs=[hbm] * (len(values) + len(earlier)),
        out_specs=[hbm] * len(values),
        input_output_aliases={i: i for i in range(len(values))},
        compiler_params=pltpu.CompilerParams(vmem_limit_bytes=1024 * 1024),
        cost_estimate=pl.CostEstimate(flops=0, bytes_accessed=0, transcendentals=0),
    )(*values, *earlier)


def on_device(
    tokens,
    cotangent,
    router,
    first_choice,
    second_choice,
    slot_index,
    overflow,
    weight_in,
    weight_out,
):
    experts = router.shape[1]
    token_count, width = tokens.shape
    capacity = token_count // experts
    slots = experts * capacity
    cut = slots // 2
    bf = jnp.bfloat16

    chosen = jnp.where(overflow == 0, first_choice, second_choice)
    position = jnp.where(overflow < 2, chosen * capacity + slot_index, -1)
    place = (jnp.arange(slots)[:, None] == position[None, :]).astype(bf)

    def placed(rows):
        picked = jnp.dot(place, rows, preferred_element_type=jnp.float32).astype(bf)
        return picked.reshape(experts, capacity, width)

    arrived = swap(jnp.concatenate([placed(tokens), placed(cotangent)], 1))
    arrived = arrived.reshape(2 * slots, width)
    wanted = (jnp.arange(slots) // capacity) * 2 * capacity + jnp.arange(slots) % capacity

    def pick(offset):
        chosen_rows = (wanted[:, None] + offset == jnp.arange(2 * slots)[None, :]).astype(bf)
        return jnp.dot(chosen_rows, arrived, preferred_element_type=jnp.float32).astype(bf)

    x0, c0 = pick(0), pick(capacity)

    lane = jnp.arange(LANES)
    me = lax.axis_index("expert")
    hot_first = (lane == me).astype(jnp.float32)[None, :]
    hot_all = (lane % experts == me).astype(jnp.float32)[None, :]
    position_z = lax.axis_index("tensor").astype(jnp.int32).reshape(1)
    shared = (position_z, router.T, hot_first, hot_all, weight_in[0], weight_out[0])

    def one_step(up, down):
        return downward(down), upward(up)

    total_rows = RING * slots
    flag, carry, near = run_group((x0,), (c0,), ((0, 0),), shared, None, 0, total_rows)
    shared = (*shared[:4], *near)
    x1, x7 = one_step(x0, x0)
    c1, c7 = one_step(c0, c0)
    x1, x7 = gate((x1, x7), flag)
    x2, x6 = one_step(x7, x1)
    c2, c6 = one_step(c7, c1)
    flag, carry, _ = run_group((x1, x7), (c1, c7), ((1, 0), (7, 0)), shared, carry, slots, total_rows)
    x2, x6 = gate((x2, x6), flag)
    x3, x5 = one_step(x6, x2)
    c3, c5 = one_step(c6, c2)
    flag, carry, _ = run_group((x2, x6), (c2, c6), ((2, 0), (6, 0)), shared, carry, 3 * slots, total_rows)
    x3, x5 = gate((x3, x5), flag)
    x4_low, x4_high = one_step(x5[:cut], x3[cut:])
    c4_low, c4_high = one_step(c5[:cut], c3[cut:])
    flag, carry, _ = run_group((x3, x5), (c3, c5), ((3, 0), (5, 0)), shared, carry, 5 * slots, total_rows)
    flag, carry, _ = run_group(
        (x4_high, x4_low),
        (c4_high, c4_low),
        ((4, 0), (4, cut)),
        shared,
        carry,
        7 * slots,
        total_rows,
    )
    router_term, x, scaled, activated, hidden_grad, back = carry

    weight_out_grad = contract_first(activated, scaled).astype(bf)
    weight_in_grad = contract_first(x, hidden_grad).astype(bf)
    router_sum = jnp.sum(swap(router_term), axis=0)
    for mask in (1, 2, 4):
        router_sum = router_sum + lax.ppermute(
            router_sum, "tensor", [(i, i ^ mask) for i in range(RING)]
        )

    spread = swap(jnp.broadcast_to(router_sum[None], (experts,) + router_sum.shape))
    router_grad = (
        spread.reshape(width // LANES, 2, experts // 2, LANES)
        .transpose(0, 3, 1, 2)
        .reshape(width, experts)
    )

    own = lax.psum_scatter(back, "tensor", scatter_dimension=0, tiled=True)
    (own,) = gate((own,), spread[0])
    home = swap(own.reshape(experts, capacity, width)).reshape(slots, width)
    token_grad = contract_first(place, home).astype(bf)
    return (token_grad, weight_in_grad[None], weight_out_grad[None], router_grad)


def solution(mesh):
    in_specs = (
        P(("expert", "tensor"), None),
        P(("expert", "tensor"), None),
        P(),
        P(("expert", "tensor")),
        P(("expert", "tensor")),
        P(("expert", "tensor")),
        P(("expert", "tensor")),
        P("expert", None, "tensor"),
        P("expert", "tensor", None),
    )
    out_specs = (
        P(("expert", "tensor"), None),
        P("expert", None, "tensor"),
        P("expert", "tensor", None),
        P(),
    )
    return jax.shard_map(
        on_device, mesh=mesh, in_specs=in_specs, out_specs=out_specs, check_vma=False
    )
```

```python
import functools

import jax
import jax.numpy as jnp
from jax import lax
from jax.experimental import pallas as pl
from jax.experimental.pallas import tpu as pltpu
from jax.sharding import PartitionSpec as P

RING = 8
LANES = 128


def gelu_parts(hidden):
    curve = jnp.tanh(0.7978845608 * (hidden + 0.044715 * hidden * hidden * hidden))
    shaped = 0.5 * hidden * (1.0 + curve)
    slope = 0.5 * (1.0 + curve) + 0.5 * hidden * (1.0 - curve * curve) * 0.7978845608 * (
        1.0 + 0.134145 * hidden * hidden
    )
    return (shaped, slope)


def contract_first(operand, other):
    return lax.dot_general(
        operand, other, (((0,), (0,)), ((), ())), preferred_element_type=jnp.float32
    )


def contract_last(operand, other):
    return lax.dot_general(
        operand, other, (((1,), (1,)), ((), ())), preferred_element_type=jnp.float32
    )


def upward(value):
    return lax.ppermute(value, "tensor", [(i, (i + 1) % RING) for i in range(RING)])


def downward(value):
    return lax.ppermute(value, "tensor", [(i, (i - 1) % RING) for i in range(RING)])


def swap(value):
    return lax.all_to_all(value, "expert", split_axis=0, concat_axis=0, tiled=True)


def group_kernel(
    places,
    first,
    row_start,
    experts,
    *refs,
):
    refs = list(refs)
    count = len(places)

    def take(n):
        out = refs[:n]
        del refs[:n]
        return out

    x_parts, cot_parts = take(count), take(count)
    me, router_rows, hot_first, hot_all, win, wout = take(6)
    if not first:
        (rt_prev,) = take(1)
        take(5)
    flag, rt_out, x_all, dy_all, act_all, hg_all, back_all = take(7)
    if first:
        win_far, wout_far = win, wout
        win, wout = take(2)
    xs, cots, dys, acts, hgs, terms, router_wide, router_back, in_sems, out_sems = refs
    rows, width = xs.shape
    each = rows // count
    hidden_units = acts.shape[1]

    def part(n):
        return slice(n * each, (n + 1) * each)

    fetch_x = [
        pltpu.make_async_copy(x_parts[n], xs.at[pl.ds(n * each, each), :], in_sems.at[n])
        for n in range(count)
    ]
    fetch_cot = [
        pltpu.make_async_copy(
            cot_parts[n], cots.at[pl.ds(n * each, each), :], in_sems.at[count + n]
        )
        for n in range(count)
    ]
    fetch_weights = []
    if first:
        fetch_weights = [
            pltpu.make_async_copy(win_far, win, in_sems.at[2 * count]),
            pltpu.make_async_copy(wout_far, wout, in_sems.at[2 * count + 1]),
        ]
    for copy in fetch_x + fetch_cot + fetch_weights:
        copy.start()
    flag[...] = jnp.zeros(flag.shape, flag.dtype)
    whole = router_rows[...]
    high = whole.astype(jnp.bfloat16)
    low = (whole - high.astype(jnp.float32)).astype(jnp.bfloat16)
    for n in range(LANES // experts):
        router_wide[n * experts : (n + 1) * experts, :] = high
        router_wide[LANES + n * experts : LANES + (n + 1) * experts, :] = low
        router_back[n * experts : (n + 1) * experts, :] = (high, high, low, jnp.zeros_like(low))[n]

    for copy in fetch_x:
        copy.wait()
    wide = contract_last(xs[...], router_wide[...])
    raised = jnp.exp(wide[:, :LANES] + wide[:, LANES:])
    total = jnp.sum(raised, axis=1, keepdims=True) * (experts / LANES)
    chances = raised / total
    gate = jnp.sum(chances * hot_first[...], axis=1, keepdims=True)
    for copy in fetch_cot:
        copy.wait()
    dys[...] = (gate * cots[...].astype(jnp.float32)).astype(jnp.bfloat16)

    for copy in fetch_weights:
        copy.wait()
    strength = jnp.zeros((rows, 1), jnp.float32)
    start = 0
    while start < hidden_units:
        span = slice(start, min(start + 256, hidden_units))
        shaped, slope = gelu_parts(
            jnp.dot(xs[...], win[:, span], preferred_element_type=jnp.float32)
        )
        activated = shaped.astype(jnp.bfloat16)
        act_grad = contract_last(dys[...], wout[span, :])
        acts[:, span] = activated
        hgs[:, span] = (act_grad * slope).astype(jnp.bfloat16)
        strength = strength + jnp.sum(
            activated.astype(jnp.float32) * act_grad, axis=1, keepdims=True
        )
        start += 256

    stores = [
        pltpu.make_async_copy(src, dst.at[pl.ds(row_start, rows), :], out_sems.at[i])
        for i, (src, dst) in enumerate(
            ((xs, x_all), (dys, dy_all), (acts, act_all), (hgs, hg_all))
        )
    ]
    for copy in stores:
        copy.start()

    logit_grad = strength * (hot_all[...] - chances)
    high_wide = logit_grad.astype(jnp.bfloat16).astype(jnp.float32)
    piece = lax.broadcasted_iota(jnp.int32, (rows, LANES), 1) // experts
    joined = jnp.where(
        piece == 1, logit_grad - high_wide, jnp.where(piece == 3, 0.0, high_wide)
    ).astype(jnp.bfloat16)

    for start in range(0, width, 256):
        span = slice(start, start + 256)
        term = contract_last(hgs[...], win[span, :]) + jnp.dot(
            joined, router_back[:, span], preferred_element_type=jnp.float32
        )
        terms[:, span] = term.astype(jnp.bfloat16)

    block = x_all.shape[0] // RING
    for n, (ahead, offset) in enumerate(places):
        at = pl.multiple_of(lax.rem(me[0] + ahead, RING) * block + offset, each)
        stores.append(
            pltpu.make_async_copy(
                terms.at[pl.ds(n * each, each), :],
                back_all.at[pl.ds(at, each), :],
                out_sems.at[4 + n],
            )
        )
        stores[-1].start()

    half = experts // 2
    for start in range(0, width, 256):
        both = contract_first(joined, xs[:, start : start + 256])
        summed = both[:experts] + both[experts : 2 * experts]
        for extra in range(2):
            for side in range(2):
                slot = (start // LANES + extra) * 2 + side
                value = summed[
                    side * half : (side + 1) * half, extra * LANES : (extra + 1) * LANES
                ]
                if not first:
                    value = value + rt_prev[slot]
                rt_out[slot] = value

    for copy in stores:
        copy.wait()


def run_group(x_parts, cot_parts, places, shared, carry, row_start, total_rows):
    _, router_rows, _, _, win, wout = shared
    count = len(x_parts)
    experts, width = router_rows.shape
    hidden_units = win.shape[1]
    rows = count * x_parts[0].shape[0]
    bf = jnp.bfloat16
    out_shape = [
        jax.ShapeDtypeStruct((8, LANES), jnp.float32),
        pltpu.VMEM((experts, experts // 2, LANES), jnp.float32),
        pltpu.HBM((total_rows, width), bf),
        pltpu.HBM((total_rows, width), bf),
        pltpu.HBM((total_rows, hidden_units), bf),
        pltpu.HBM((total_rows, hidden_units), bf),
        pltpu.HBM((total_rows, width), bf),
    ]
    vmem = pl.BlockSpec(memory_space=pltpu.VMEM)
    hbm = pl.BlockSpec(memory_space=pltpu.HBM)
    first = carry is None
    parts = (*x_parts, *cot_parts)
    parts = [pltpu.with_memory_space_constraint(part, pltpu.VMEM) for part in parts]
    if first:
        weights = [pltpu.with_memory_space_constraint(part, pltpu.HBM) for part in (win, wout)]
    else:
        weights = [win, wout]
    operands = [*parts, *shared[:4], *weights]
    in_specs = [vmem] * (2 * count)
    in_specs += [pl.BlockSpec(memory_space=pltpu.SMEM), vmem, vmem, vmem]
    in_specs += [hbm if first else vmem] * 2
    out_specs = [vmem, vmem] + [hbm] * 5
    aliases = {}
    if first:
        out_shape += [pltpu.VMEM(win.shape, bf), pltpu.VMEM(wout.shape, bf)]
        out_specs += [vmem, vmem]
    else:
        base = len(operands)
        operands.append(carry[0])
        operands += [pltpu.with_memory_space_constraint(part, pltpu.HBM) for part in carry[1:]]
        in_specs += [vmem] + [hbm] * 5
        aliases = {base + 1 + i: 2 + i for i in range(5)}
    out = pl.pallas_call(
        functools.partial(group_kernel, places, first, row_start, experts),
        out_shape=out_shape,
        in_specs=in_specs,
        out_specs=out_specs,
        input_output_aliases=aliases,
        scratch_shapes=[
            pltpu.VMEM((rows, width), bf),
            pltpu.VMEM((rows, width), bf),
            pltpu.VMEM((rows, width), bf),
            pltpu.VMEM((rows, hidden_units), bf),
            pltpu.VMEM((rows, hidden_units), bf),
            pltpu.VMEM((rows, width), bf),
            pltpu.VMEM((2 * LANES, width), bf),
            pltpu.VMEM((LANES, width), bf),
            pltpu.SemaphoreType.DMA((2 * count + 2,)),
            pltpu.SemaphoreType.DMA((4 + count,)),
        ],
        compiler_params=pltpu.CompilerParams(vmem_limit_bytes=16 * 1024 * 1024),
        cost_estimate=pl.CostEstimate(
            flops=2 * rows * width * (hidden_units * 3 + 512),
            bytes_accessed=4 * 1024 * 1024,
            transcendentals=rows * hidden_units,
        ),
    )(*operands)
    return out[0], out[1:7], out[7:]


def gate(values, *earlier):
    hbm = pl.BlockSpec(memory_space=pltpu.HBM)
    return pl.pallas_call(
        lambda *refs: None,
        out_shape=[jax.ShapeDtypeStruct(value.shape, value.dtype) for value in values],
        in_specs=[hbm] * (len(values) + len(earlier)),
        out_specs=[hbm] * len(values),
        input_output_aliases={i: i for i in range(len(values))},
        compiler_params=pltpu.CompilerParams(vmem_limit_bytes=1024 * 1024),
        cost_estimate=pl.CostEstimate(flops=0, bytes_accessed=0, transcendentals=0),
    )(*values, *earlier)


def pack_kernel(capacity, *refs):
    out, near, sems = refs[6], refs[7:13], refs[13]
    copies = [
        pltpu.make_async_copy(src, dst, sems.at[i])
        for i, (src, dst) in enumerate(zip(refs[:6], near))
    ]
    for copy in copies:
        copy.start()
    for copy in copies:
        copy.wait()
    first, second, slot, overflow, tokens, cotangent = near
    rows, count = out.shape[0], tokens.shape[0]
    chosen = jnp.where(overflow[...] == 0, first[...], second[...])
    position = jnp.where(overflow[...] < 2, chosen * capacity + slot[...], -1)
    row = lax.broadcasted_iota(jnp.int32, (rows, count), 0)
    within = row % (2 * capacity)
    hit = (row // (2 * capacity)) * capacity + within % capacity == position
    ones = jnp.where(hit, 1.0, 0.0)
    take_tokens = jnp.where(within < capacity, ones, 0.0).astype(jnp.bfloat16)
    take_cot = jnp.where(within < capacity, 0.0, ones).astype(jnp.bfloat16)
    for start in range(0, tokens.shape[1], 512):
        span = slice(start, start + 512)
        out[:, span] = (
            jnp.dot(take_tokens, tokens[:, span], preferred_element_type=jnp.float32)
            + jnp.dot(take_cot, cotangent[:, span], preferred_element_type=jnp.float32)
        ).astype(jnp.bfloat16)


def pick_kernel(capacity, arrived, x_out, cot_out):
    slots, rows = x_out.shape[0], arrived.shape[0]
    row = lax.broadcasted_iota(jnp.int32, (slots, rows), 0)
    column = lax.broadcasted_iota(jnp.int32, (slots, rows), 1)
    wanted = (row // capacity) * (2 * capacity) + row % capacity
    for out, offset in ((x_out, 0), (cot_out, capacity)):
        chosen = jnp.where(wanted + offset == column, 1.0, 0.0).astype(jnp.bfloat16)
        for start in range(0, arrived.shape[1], 512):
            span = slice(start, start + 512)
            out[:, span] = jnp.dot(
                chosen, arrived[:, span], preferred_element_type=jnp.float32
            ).astype(jnp.bfloat16)


def on_device(
    tokens,
    cotangent,
    router,
    first_choice,
    second_choice,
    slot_index,
    overflow,
    weight_in,
    weight_out,
):
    experts = router.shape[1]
    token_count, width = tokens.shape
    capacity = token_count // experts
    slots = experts * capacity
    cut = slots // 2
    bf = jnp.bfloat16

    chosen = jnp.where(overflow == 0, first_choice, second_choice)
    position = jnp.where(overflow < 2, chosen * capacity + slot_index, -1)
    place = (jnp.arange(slots)[:, None] == position[None, :]).astype(bf)

    small = pltpu.CompilerParams(vmem_limit_bytes=8 * 1024 * 1024)
    choices = [c.reshape(1, -1) for c in (first_choice, second_choice, slot_index, overflow)]
    whole = [*choices, tokens, cotangent]
    packed = pl.pallas_call(
        functools.partial(pack_kernel, capacity),
        out_shape=jax.ShapeDtypeStruct((2 * slots, width), bf),
        in_specs=[pl.BlockSpec(memory_space=pltpu.HBM)] * len(whole),
        scratch_shapes=[pltpu.VMEM(a.shape, a.dtype) for a in whole]
        + [pltpu.SemaphoreType.DMA((len(whole),))],
        compiler_params=small,
    )(*[pltpu.with_memory_space_constraint(a, pltpu.HBM) for a in whole])
    arrived = swap(packed.reshape(experts, 2 * capacity, width)).reshape(2 * slots, width)
    x0, c0 = pl.pallas_call(
        functools.partial(pick_kernel, capacity),
        out_shape=[pltpu.VMEM((slots, width), bf)] * 2,
        compiler_params=small,
    )(arrived)

    lane = jnp.arange(LANES)
    me = lax.axis_index("expert")
    hot_first = (lane == me).astype(jnp.float32)[None, :]
    hot_all = (lane % experts == me).astype(jnp.float32)[None, :]
    position_z = lax.axis_index("tensor").astype(jnp.int32).reshape(1)
    shared = (position_z, router.T, hot_first, hot_all, weight_in[0], weight_out[0])

    def one_step(up, down):
        return downward(down), upward(up)

    total_rows = RING * slots
    flag, carry, near = run_group((x0,), (c0,), ((0, 0),), shared, None, 0, total_rows)
    shared = (*shared[:4], *near)
    x1, x7 = one_step(x0, x0)
    c1, c7 = one_step(c0, c0)
    x1, x7 = gate((x1, x7), flag)
    x2, x6 = one_step(x7, x1)
    c2, c6 = one_step(c7, c1)
    flag, carry, _ = run_group((x1, x7), (c1, c7), ((1, 0), (7, 0)), shared, carry, slots, total_rows)
    x2, x6 = gate((x2, x6), flag)
    x3, x5 = one_step(x6, x2)
    c3, c5 = one_step(c6, c2)
    flag, carry, _ = run_group((x2, x6), (c2, c6), ((2, 0), (6, 0)), shared, carry, 3 * slots, total_rows)
    x3, x5 = gate((x3, x5), flag)
    x4_low, x4_high = one_step(x5[:cut], x3[cut:])
    c4_low, c4_high = one_step(c5[:cut], c3[cut:])
    flag, carry, _ = run_group((x3, x5), (c3, c5), ((3, 0), (5, 0)), shared, carry, 5 * slots, total_rows)
    flag, carry, _ = run_group(
        (x4_high, x4_low),
        (c4_high, c4_low),
        ((4, 0), (4, cut)),
        shared,
        carry,
        7 * slots,
        total_rows,
    )
    router_term, x, scaled, activated, hidden_grad, back = carry

    weight_out_grad = contract_first(activated, scaled).astype(bf)
    weight_in_grad = contract_first(x, hidden_grad).astype(bf)
    router_sum = jnp.sum(swap(router_term), axis=0)
    for mask in (1, 2, 4):
        router_sum = router_sum + lax.ppermute(
            router_sum, "tensor", [(i, i ^ mask) for i in range(RING)]
        )

    spread = swap(jnp.broadcast_to(router_sum[None], (experts,) + router_sum.shape))
    router_grad = (
        spread.reshape(width // LANES, 2, experts // 2, LANES)
        .transpose(0, 3, 1, 2)
        .reshape(width, experts)
    )

    own = lax.psum_scatter(back, "tensor", scatter_dimension=0, tiled=True)
    home = swap(own.reshape(experts, capacity, width)).reshape(slots, width)
    token_grad = contract_first(place, home).astype(bf)
    return (token_grad, weight_in_grad[None], weight_out_grad[None], router_grad)


def solution(mesh):
    in_specs = (
        P(("expert", "tensor"), None),
        P(("expert", "tensor"), None),
        P(),
        P(("expert", "tensor")),
        P(("expert", "tensor")),
        P(("expert", "tensor")),
        P(("expert", "tensor")),
        P("expert", None, "tensor"),
        P("expert", "tensor", None),
    )
    out_specs = (
        P(("expert", "tensor"), None),
        P("expert", None, "tensor"),
        P("expert", "tensor", None),
        P(),
    )
    return jax.shard_map(
        on_device, mesh=mesh, in_specs=in_specs, out_specs=out_specs, check_vma=False
    )
```

```python
import functools

import jax
import jax.numpy as jnp
from jax import lax
from jax.experimental import pallas as pl
from jax.experimental.pallas import tpu as pltpu
from jax.sharding import PartitionSpec as P

RING = 8
LANES = 128


def gelu_parts(hidden):
    curve = jnp.tanh(0.7978845608 * (hidden + 0.044715 * hidden * hidden * hidden))
    shaped = 0.5 * hidden * (1.0 + curve)
    slope = 0.5 * (1.0 + curve) + 0.5 * hidden * (1.0 - curve * curve) * 0.7978845608 * (
        1.0 + 0.134145 * hidden * hidden
    )
    return (shaped, slope)


def contract_first(operand, other):
    return lax.dot_general(
        operand, other, (((0,), (0,)), ((), ())), preferred_element_type=jnp.float32
    )


def contract_last(operand, other):
    return lax.dot_general(
        operand, other, (((1,), (1,)), ((), ())), preferred_element_type=jnp.float32
    )


def upward(value):
    return lax.ppermute(value, "tensor", [(i, (i + 1) % RING) for i in range(RING)])


def downward(value):
    return lax.ppermute(value, "tensor", [(i, (i - 1) % RING) for i in range(RING)])


def swap(value):
    return lax.all_to_all(value, "expert", split_axis=0, concat_axis=0, tiled=True)


def group_kernel(
    places,
    first,
    row_start,
    experts,
    *refs,
):
    refs = list(refs)
    count = len(places)

    def take(n):
        out = refs[:n]
        del refs[:n]
        return out

    x_parts, cot_parts = take(count), take(count)
    me, router_rows, hot_first, hot_all, win, wout = take(6)
    if not first:
        (rt_prev,) = take(1)
        take(5)
    flag, rt_out, x_all, dy_all, act_all, hg_all, back_all = take(7)
    if first:
        win_far, wout_far = win, wout
        win, wout = take(2)
    xs, dys, acts, hgs, terms, router_wide, router_back, in_sems, out_sems = refs
    rows, width = xs.shape
    each = rows // count
    hidden_units = acts.shape[1]

    def part(n):
        return slice(n * each, (n + 1) * each)

    fetch_weights = []
    if first:
        fetch_weights = [
            pltpu.make_async_copy(win_far, win, in_sems.at[0]),
            pltpu.make_async_copy(wout_far, wout, in_sems.at[1]),
        ]
    for copy in fetch_weights:
        copy.start()
    for n in range(count):
        xs[part(n), :] = x_parts[n][...]
    flag[...] = jnp.zeros(flag.shape, flag.dtype)
    whole = router_rows[...]
    high = whole.astype(jnp.bfloat16)
    low = (whole - high.astype(jnp.float32)).astype(jnp.bfloat16)
    for n in range(LANES // experts):
        router_wide[n * experts : (n + 1) * experts, :] = high
        router_wide[LANES + n * experts : LANES + (n + 1) * experts, :] = low
        router_back[n * experts : (n + 1) * experts, :] = (high, high, low, jnp.zeros_like(low))[n]

    wide = contract_last(xs[...], router_wide[...])
    raised = jnp.exp(wide[:, :LANES] + wide[:, LANES:])
    total = jnp.sum(raised, axis=1, keepdims=True) * (experts / LANES)
    chances = raised / total
    gate = jnp.sum(chances * hot_first[...], axis=1, keepdims=True)
    for n in range(count):
        dys[part(n), :] = (gate[part(n)] * cot_parts[n][...].astype(jnp.float32)).astype(
            jnp.bfloat16
        )

    for copy in fetch_weights:
        copy.wait()
    strength = jnp.zeros((rows, 1), jnp.float32)
    start = 0
    while start < hidden_units:
        span = slice(start, min(start + 256, hidden_units))
        shaped, slope = gelu_parts(
            jnp.dot(xs[...], win[:, span], preferred_element_type=jnp.float32)
        )
        activated = shaped.astype(jnp.bfloat16)
        act_grad = contract_last(dys[...], wout[span, :])
        acts[:, span] = activated
        hgs[:, span] = (act_grad * slope).astype(jnp.bfloat16)
        strength = strength + jnp.sum(
            activated.astype(jnp.float32) * act_grad, axis=1, keepdims=True
        )
        start += 256

    stores = [
        pltpu.make_async_copy(src, dst.at[pl.ds(row_start, rows), :], out_sems.at[i])
        for i, (src, dst) in enumerate(
            ((xs, x_all), (dys, dy_all), (acts, act_all), (hgs, hg_all))
        )
    ]
    for copy in stores:
        copy.start()

    logit_grad = strength * (hot_all[...] - chances)
    high_wide = logit_grad.astype(jnp.bfloat16).astype(jnp.float32)
    piece = lax.broadcasted_iota(jnp.int32, (rows, LANES), 1) // experts
    joined = jnp.where(
        piece == 1, logit_grad - high_wide, jnp.where(piece == 3, 0.0, high_wide)
    ).astype(jnp.bfloat16)

    half = experts // 2
    for start in range(0, width, 256):
        both = contract_first(joined, xs[:, start : start + 256])
        summed = both[:experts] + both[experts : 2 * experts]
        for extra in range(2):
            for side in range(2):
                slot = (start // LANES + extra) * 2 + side
                value = summed[
                    side * half : (side + 1) * half, extra * LANES : (extra + 1) * LANES
                ]
                if not first:
                    value = value + rt_prev[slot]
                rt_out[slot] = value

    for start in range(0, width, 256):
        span = slice(start, start + 256)
        term = contract_last(hgs[...], win[span, :]) + jnp.dot(
            joined, router_back[:, span], preferred_element_type=jnp.float32
        )
        terms[:, span] = term.astype(jnp.bfloat16)

    block = x_all.shape[0] // RING
    for n, (ahead, offset) in enumerate(places):
        at = pl.multiple_of(lax.rem(me[0] + ahead, RING) * block + offset, each)
        stores.append(
            pltpu.make_async_copy(
                terms.at[pl.ds(n * each, each), :],
                back_all.at[pl.ds(at, each), :],
                out_sems.at[4 + n],
            )
        )
        stores[-1].start()

    for copy in stores:
        copy.wait()


def run_group(x_parts, cot_parts, places, shared, carry, row_start, total_rows):
    _, router_rows, _, _, win, wout = shared
    count = len(x_parts)
    experts, width = router_rows.shape
    hidden_units = win.shape[1]
    rows = count * x_parts[0].shape[0]
    bf = jnp.bfloat16
    out_shape = [
        jax.ShapeDtypeStruct((8, LANES), jnp.float32),
        pltpu.VMEM((experts, experts // 2, LANES), jnp.float32),
        pltpu.HBM((total_rows, width), bf),
        pltpu.HBM((total_rows, width), bf),
        pltpu.HBM((total_rows, hidden_units), bf),
        pltpu.HBM((total_rows, hidden_units), bf),
        pltpu.HBM((total_rows, width), bf),
    ]
    vmem = pl.BlockSpec(memory_space=pltpu.VMEM)
    hbm = pl.BlockSpec(memory_space=pltpu.HBM)
    first = carry is None
    parts = (*x_parts, *cot_parts)
    parts = [pltpu.with_memory_space_constraint(part, pltpu.VMEM) for part in parts]
    if first:
        weights = [pltpu.with_memory_space_constraint(part, pltpu.HBM) for part in (win, wout)]
    else:
        weights = [win, wout]
    operands = [*parts, *shared[:4], *weights]
    in_specs = [vmem] * (2 * count)
    in_specs += [pl.BlockSpec(memory_space=pltpu.SMEM), vmem, vmem, vmem]
    in_specs += [hbm if first else vmem] * 2
    out_specs = [vmem, vmem] + [hbm] * 5
    aliases = {}
    if first:
        out_shape += [pltpu.VMEM(win.shape, bf), pltpu.VMEM(wout.shape, bf)]
        out_specs += [vmem, vmem]
    else:
        base = len(operands)
        operands.append(carry[0])
        operands += [pltpu.with_memory_space_constraint(part, pltpu.HBM) for part in carry[1:]]
        in_specs += [vmem] + [hbm] * 5
        aliases = {base + 1 + i: 2 + i for i in range(5)}
    out = pl.pallas_call(
        functools.partial(group_kernel, places, first, row_start, experts),
        out_shape=out_shape,
        in_specs=in_specs,
        out_specs=out_specs,
        input_output_aliases=aliases,
        scratch_shapes=[
            pltpu.VMEM((rows, width), bf),
            pltpu.VMEM((rows, width), bf),
            pltpu.VMEM((rows, hidden_units), bf),
            pltpu.VMEM((rows, hidden_units), bf),
            pltpu.VMEM((rows, width), bf),
            pltpu.VMEM((2 * LANES, width), bf),
            pltpu.VMEM((LANES, width), bf),
            pltpu.SemaphoreType.DMA((2,)),
            pltpu.SemaphoreType.DMA((4 + count,)),
        ],
        compiler_params=pltpu.CompilerParams(vmem_limit_bytes=16 * 1024 * 1024),
        cost_estimate=pl.CostEstimate(
            flops=2 * rows * width * (hidden_units * 3 + 512),
            bytes_accessed=4 * 1024 * 1024,
            transcendentals=rows * hidden_units,
        ),
    )(*operands)
    return out[0], out[1:7], out[7:]


def gate(values, *earlier):
    hbm = pl.BlockSpec(memory_space=pltpu.HBM)
    return pl.pallas_call(
        lambda *refs: None,
        out_shape=[jax.ShapeDtypeStruct(value.shape, value.dtype) for value in values],
        in_specs=[hbm] * (len(values) + len(earlier)),
        out_specs=[hbm] * len(values),
        input_output_aliases={i: i for i in range(len(values))},
        compiler_params=pltpu.CompilerParams(vmem_limit_bytes=1024 * 1024),
        cost_estimate=pl.CostEstimate(flops=0, bytes_accessed=0, transcendentals=0),
    )(*values, *earlier)


def pack_kernel(capacity, *refs):
    out, near, sems = refs[6], refs[7:13], refs[13]
    copies = [
        pltpu.make_async_copy(src, dst, sems.at[i])
        for i, (src, dst) in enumerate(zip(refs[:6], near))
    ]
    for copy in copies:
        copy.start()
    for copy in copies:
        copy.wait()
    first, second, slot, overflow, tokens, cotangent = near
    rows, count = out.shape[0], tokens.shape[0]
    chosen = jnp.where(overflow[...] == 0, first[...], second[...])
    position = jnp.where(overflow[...] < 2, chosen * capacity + slot[...], -1)
    row = lax.broadcasted_iota(jnp.int32, (rows, count), 0)
    within = row % (2 * capacity)
    hit = (row // (2 * capacity)) * capacity + within % capacity == position
    ones = jnp.where(hit, 1.0, 0.0)
    take_tokens = jnp.where(within < capacity, ones, 0.0).astype(jnp.bfloat16)
    take_cot = jnp.where(within < capacity, 0.0, ones).astype(jnp.bfloat16)
    for start in range(0, tokens.shape[1], 512):
        span = slice(start, start + 512)
        out[:, span] = (
            jnp.dot(take_tokens, tokens[:, span], preferred_element_type=jnp.float32)
            + jnp.dot(take_cot, cotangent[:, span], preferred_element_type=jnp.float32)
        ).astype(jnp.bfloat16)


def pick_kernel(capacity, arrived, x_out, cot_out):
    slots, rows = x_out.shape[0], arrived.shape[0]
    row = lax.broadcasted_iota(jnp.int32, (slots, rows), 0)
    column = lax.broadcasted_iota(jnp.int32, (slots, rows), 1)
    wanted = (row // capacity) * (2 * capacity) + row % capacity
    for out, offset in ((x_out, 0), (cot_out, capacity)):
        chosen = jnp.where(wanted + offset == column, 1.0, 0.0).astype(jnp.bfloat16)
        for start in range(0, arrived.shape[1], 512):
            span = slice(start, start + 512)
            out[:, span] = jnp.dot(
                chosen, arrived[:, span], preferred_element_type=jnp.float32
            ).astype(jnp.bfloat16)


def on_device(
    tokens,
    cotangent,
    router,
    first_choice,
    second_choice,
    slot_index,
    overflow,
    weight_in,
    weight_out,
):
    experts = router.shape[1]
    token_count, width = tokens.shape
    capacity = token_count // experts
    slots = experts * capacity
    cut = slots // 2
    bf = jnp.bfloat16

    chosen = jnp.where(overflow == 0, first_choice, second_choice)
    position = jnp.where(overflow < 2, chosen * capacity + slot_index, -1)
    place = (jnp.arange(slots)[:, None] == position[None, :]).astype(bf)

    small = pltpu.CompilerParams(vmem_limit_bytes=8 * 1024 * 1024)
    choices = [c.reshape(1, -1) for c in (first_choice, second_choice, slot_index, overflow)]
    whole = [*choices, tokens, cotangent]
    packed = pl.pallas_call(
        functools.partial(pack_kernel, capacity),
        out_shape=jax.ShapeDtypeStruct((2 * slots, width), bf),
        in_specs=[pl.BlockSpec(memory_space=pltpu.HBM)] * len(whole),
        scratch_shapes=[pltpu.VMEM(a.shape, a.dtype) for a in whole]
        + [pltpu.SemaphoreType.DMA((len(whole),))],
        compiler_params=small,
    )(*[pltpu.with_memory_space_constraint(a, pltpu.HBM) for a in whole])
    arrived = swap(packed.reshape(experts, 2 * capacity, width)).reshape(2 * slots, width)
    x0, c0 = pl.pallas_call(
        functools.partial(pick_kernel, capacity),
        out_shape=[pltpu.VMEM((slots, width), bf)] * 2,
        compiler_params=small,
    )(arrived)

    lane = jnp.arange(LANES)
    me = lax.axis_index("expert")
    hot_first = (lane == me).astype(jnp.float32)[None, :]
    hot_all = (lane % experts == me).astype(jnp.float32)[None, :]
    position_z = lax.axis_index("tensor").astype(jnp.int32).reshape(1)
    shared = (position_z, router.T, hot_first, hot_all, weight_in[0], weight_out[0])

    def one_step(up, down):
        return downward(down), upward(up)

    total_rows = RING * slots
    flag, carry, near = run_group((x0,), (c0,), ((0, 0),), shared, None, 0, total_rows)
    shared = (*shared[:4], *near)
    x1, x7 = one_step(x0, x0)
    c1, c7 = one_step(c0, c0)
    x1, x7 = gate((x1, x7), flag)
    x2, x6 = one_step(x7, x1)
    c2, c6 = one_step(c7, c1)
    flag, carry, _ = run_group((x1, x7), (c1, c7), ((1, 0), (7, 0)), shared, carry, slots, total_rows)
    x2, x6 = gate((x2, x6), flag)
    x3, x5 = one_step(x6, x2)
    c3, c5 = one_step(c6, c2)
    flag, carry, _ = run_group((x2, x6), (c2, c6), ((2, 0), (6, 0)), shared, carry, 3 * slots, total_rows)
    x3, x5 = gate((x3, x5), flag)
    x4_low, x4_high = one_step(x5[:cut], x3[cut:])
    c4_low, c4_high = one_step(c5[:cut], c3[cut:])
    flag, carry, _ = run_group((x3, x5), (c3, c5), ((3, 0), (5, 0)), shared, carry, 5 * slots, total_rows)
    flag, carry, _ = run_group(
        (x4_high, x4_low),
        (c4_high, c4_low),
        ((4, 0), (4, cut)),
        shared,
        carry,
        7 * slots,
        total_rows,
    )
    router_term, x, scaled, activated, hidden_grad, back = carry

    weight_out_grad = contract_first(activated, scaled).astype(bf)
    weight_in_grad = contract_first(x, hidden_grad).astype(bf)
    router_sum = jnp.sum(swap(router_term), axis=0)
    for mask in (1, 2, 4):
        router_sum = router_sum + lax.ppermute(
            router_sum, "tensor", [(i, i ^ mask) for i in range(RING)]
        )

    spread = swap(jnp.broadcast_to(router_sum[None], (experts,) + router_sum.shape))
    router_grad = (
        spread.reshape(width // LANES, 2, experts // 2, LANES)
        .transpose(0, 3, 1, 2)
        .reshape(width, experts)
    )

    own = lax.psum_scatter(back, "tensor", scatter_dimension=0, tiled=True)
    home = swap(own.reshape(experts, capacity, width)).reshape(slots, width)
    token_grad = contract_first(place, home).astype(bf)
    return (token_grad, weight_in_grad[None], weight_out_grad[None], router_grad)


def solution(mesh):
    in_specs = (
        P(("expert", "tensor"), None),
        P(("expert", "tensor"), None),
        P(),
        P(("expert", "tensor")),
        P(("expert", "tensor")),
        P(("expert", "tensor")),
        P(("expert", "tensor")),
        P("expert", None, "tensor"),
        P("expert", "tensor", None),
    )
    out_specs = (
        P(("expert", "tensor"), None),
        P("expert", None, "tensor"),
        P("expert", "tensor", None),
        P(),
    )
    return jax.shard_map(
        on_device, mesh=mesh, in_specs=in_specs, out_specs=out_specs, check_vma=False
    )
```
